32 devices in a mesh: group: 2 (over x), link: 16 (over z, y, core).
Axes of the slice: x: 2, y: 2, z: 4, core: 2. Of those that a mesh axis runs over, the one named last changes fastest.
Arguments:
- ray_rows: float32 [16384, 128], P(('group', 'link')), parts along dimension 0, may hold values from -6 to 6
- visible: int32 [256, 256], P(('group', 'link')), parts along dimension 0, may hold values from 0 to 8191, as said below
- base_tap: int32 [256, 256], P(('group', 'link')), parts along dimension 0, may hold values from 0 to 63
- frac_index: int32 [256, 256], P(('group', 'link')), parts along dimension 0, may hold values from 0 to 15
- elem_tap: int32 [8, 2048], P(None, 'link'), may hold values from 0 to 1073741823
- elem_gain: float32 [8, 2048], P(None, 'link'), may hold values from -0.375 to 0.375
Outputs:
- received: float32 [256, 2048, 128], P(('group', 'link')), parts along dimension 0
The draws below stay inside these ranges and needn't reach their ends.
There are 2 independent parts, one for each index of `group`. The reference program is written for one: setup_inputs(seed, part) draws one part's arguments, and reference() takes and returns one part's arrays. A program takes and returns all parts, laid end to end along the dimension named above; an argument that names none is the same for every part. Nothing has to cross between parts.
Inputs may be any that keep to these rules, and one draw needn't show every extreme that they name: `visible`: scatterer s is owned by link device s // 512. Among the 2048 entries of the UEs of one device (aligned blocks of 8 rows), at most 256 name scatterers of any one owner, and some owner is named exactly 256 times in every block. An id may repeat. Scatterer ids and other integer indices may be sent packed several to a 32-bit word; this is the one exception to the rule of bits below.
All inputs are finite; a program needn't handle non-finite values.
Results may differ from the reference program's by a relative error of at most 0.000073.
Values sent between devices are 32-bit elements; how exact they have to be, the bound alone decides.
A program may use at most 512 MiB of HBM per device.

```python
import jax
import jax.numpy as jnp
import numpy as np
from jax import lax

RAY_LEN = 128
ELEMS = 2048
SAMPLES = 128
TAP_SPAN = 32
BASE_SPAN = 64
FRACS = 16
CLUSTERS = 8
VIS = 256
UE_DEV = 8
SC_DEV = 512
UES = 128
SCAT = 8192
N_LINK = 16


def draw_visible(key, part):
    key = jax.random.fold_in(key, 7)
    entries = UE_DEV * VIS
    share_mean = entries // N_LINK
    quarter = N_LINK // 4
    counts = np.array([2 * share_mean] * quarter + [share_mean] * (N_LINK // 2) + [0] * (N_LINK - quarter - N_LINK // 2))
    rank_list = jnp.asarray(np.repeat(np.arange(N_LINK), counts), jnp.int32)

    def one_block(block_key):
        key_one, key_two, key_three = jax.random.split(block_key, 3)
        shuffle_owner = jax.random.permutation(key_one, N_LINK).astype(jnp.int32)
        owner_list = shuffle_owner[rank_list]
        reorder = jax.random.permutation(key_two, entries)
        owner_list = owner_list[reorder]
        within = jax.random.randint(key_three, (entries,), 0, SC_DEV).astype(jnp.int32)
        return (owner_list * SC_DEV + within).reshape(UE_DEV, VIS)
    key_list = jax.random.split(key, N_LINK)
    return jax.vmap(one_block)(key_list).reshape(UE_DEV * N_LINK, VIS).astype(jnp.int32)


def set_ends(values, own_key, smallest, largest):
    spot = [jax.random.randint(jax.random.fold_in(own_key, axis), (), 0, length) for axis, length in enumerate(values.shape)]
    longest = values.shape.index(max(values.shape))
    neighbour = spot[:longest] + [(spot[longest] + 1) % values.shape[longest]] + spot[longest + 1:]
    return values.at[tuple(spot)].set(smallest).at[tuple(neighbour)].set(largest)


def block_scale(stream_key, shape, cuts, smallest, largest):
    def one(dim, blocks):
        draws = jax.random.uniform(jax.random.fold_in(jax.random.fold_in(stream_key, 6), dim), (blocks,), jnp.float32, smallest / len(cuts), largest / len(cuts))
        return jnp.repeat(jnp.exp(draws), shape[dim] // blocks).reshape((-1,) + (1,) * (len(shape) - dim - 1))

    loudness = one(*cuts[0])
    for cut in cuts[1:]:
        loudness = loudness * one(*cut)
    return loudness


def centred(key, extent, scale, reach, pieces=(), held_as=jnp.bfloat16):
    result = scale * jax.random.normal(key, extent, jnp.float32)
    if pieces:
        result = result * block_scale(key, extent, pieces, -0.22, 0.18)
    return jnp.clip(result, -reach, reach).astype(held_as)


def setup_inputs(seed: int = 0, part: int = 0) -> dict:
    arg_keys = jax.random.split(jax.random.key(seed), 7)
    part_keys = jax.random.split(jax.random.fold_in(arg_keys[6], part), 7)
    ray_rows = centred(part_keys[0], (SCAT, RAY_LEN), 1.0, 6.0, ((0, 16),), jnp.float32)
    visible = draw_visible(jax.random.fold_in(jax.random.fold_in(arg_keys[6], part), 71), part)
    base_tap = set_ends(jax.random.randint(part_keys[2], (UES, VIS), 0, BASE_SPAN), jax.random.fold_in(part_keys[2], 1), 0, BASE_SPAN - 1).astype(jnp.int32)
    frac_index = set_ends(jax.random.randint(part_keys[3], (UES, VIS), 0, FRACS), jax.random.fold_in(part_keys[3], 1), 0, FRACS - 1).astype(jnp.int32)
    elem_tap = set_ends(jax.random.randint(arg_keys[4], (CLUSTERS, ELEMS), 0, 1073741824), jax.random.fold_in(arg_keys[4], 1), 0, 1073741823).astype(jnp.int32)
    elem_gain = centred(arg_keys[5], (CLUSTERS, ELEMS), (VIS ** -0.5), 0.375, ((1, 16),), jnp.float32)
    return {"ray_rows": ray_rows, "visible": visible, "base_tap": base_tap, "frac_index": frac_index, "elem_tap": elem_tap, "elem_gain": elem_gain}


def lagrange(frac_flat):
    mu_val = frac_flat.astype(jnp.float32) / FRACS
    first = -mu_val * (mu_val - 1.0) * (mu_val - 2.0) / 6.0
    second = (mu_val + 1.0) * (mu_val - 1.0) * (mu_val - 2.0) / 2.0
    third = -(mu_val + 1.0) * mu_val * (mu_val - 2.0) / 2.0
    fourth = (mu_val + 1.0) * mu_val * (mu_val - 1.0) / 6.0
    return jnp.stack([first, second, third, fourth], axis=1)


def farrow_place(picked, frac_index, base_tap):
    coeffs = lagrange(frac_index.reshape(-1))
    length = picked.shape[1]
    padded = jnp.pad(picked, ((0, 0), (3, 3)))
    filtered = jnp.zeros((picked.shape[0], length + 3), jnp.float32)
    for shift_k in range(4):
        filtered = filtered + coeffs[:, shift_k:shift_k + 1] * padded[:, 3 - shift_k:3 - shift_k + length + 3]
    width = SAMPLES + TAP_SPAN
    offsets = jnp.arange(width).astype(jnp.int32)[None, :] - base_tap.reshape(-1, 1).astype(jnp.int32)
    inside = (offsets >= 0) & (offsets < length + 3)
    placed = jnp.take_along_axis(filtered, jnp.clip(offsets, 0, length + 2), axis=1)
    return jnp.where(inside, placed, jnp.float32(0.0))


def cluster_sum(placed, visible):
    member = ((visible % CLUSTERS)[:, :, None] == jnp.arange(CLUSTERS).astype(jnp.int32)[None, None, :]).astype(jnp.float32)
    shaped = placed.reshape(visible.shape[0], visible.shape[1], -1)
    return jnp.einsum('uvc,uvw->ucw', member, shaped, precision=lax.Precision.HIGHEST)


def pick_line(values_row, spot_list):
    return values_row[spot_list]


def element_sum(zones, elem_tap, elem_gain):
    reduced_tap = (elem_tap % TAP_SPAN).astype(jnp.int32)
    positions = jnp.arange(SAMPLES).astype(jnp.int32)[None, None, :] + TAP_SPAN - reduced_tap[:, :, None]

    def one_user(zone_rows):
        gathered = jax.vmap(pick_line)(zone_rows, positions)
        return jnp.einsum('ce,ces->es', elem_gain, gathered, precision=lax.Precision.HIGHEST)

    return lax.map(one_user, zones)


def reference(ray_rows, visible, base_tap, frac_index, elem_tap, elem_gain):
    picked = ray_rows[visible.reshape(-1)]
    placed = farrow_place(picked, frac_index, base_tap)
    zones = cluster_sum(placed, visible)
    return element_sum(zones, elem_tap, elem_gain)
```

```python
import functools

import jax
import jax.numpy as jnp
from jax import lax
from jax.experimental import pallas as pl
from jax.experimental.pallas import tpu as pltpu
from jax.sharding import PartitionSpec as P

SAMPLES = 128
TAP_SPAN = 32
BASE_SPAN = 64
FRACS = 16
CLUSTERS = 8
LANES = 128
TAPS = 4
PLACE_ROWS = -(-(BASE_SPAN + TAPS - 1) * CLUSTERS // 16) * 16
SETS = 2

F32 = jnp.float32
BF16 = jnp.bfloat16


def flip(value, mask):
    result = value
    bit = 1
    while bit <= mask:
        if mask & bit:
            result = result + bit * (1 - 2 * ((value // bit) % 2))
        bit *= 2
    return result


def split(value):
    high = value.astype(BF16)
    return high, (value - high.astype(F32)).astype(BF16)


def zone_kernel(
    n, sets,
    ray_ref, vis_ref, base_ref, frac_ref, tap_ref, gain_ref,
    zone_ref, elem_ref,
    rays, elem_all, meta_own, meta_all, id_cols, ray_split, picked, zone_part, zone_got,
    ray_send, ray_recv, fwd_send, fwd_recv, meta_send, meta_recv, elem_send, elem_recv,
    zone_send, zone_recv,
):
    per_set = n // sets
    chips = per_set // 2
    me = lax.axis_index("link")
    own_set = me // per_set
    place = me % per_set
    chip = place // 2
    core = place % 2
    sibling = me + 1 - 2 * core
    users, slots = vis_ref.shape
    owned = ray_ref.shape[0]

    barrier = pltpu.get_barrier_semaphore()
    for step in range(1, n):
        pl.semaphore_signal(
            barrier, inc=1, device_id={"link": (me + step) % n}, device_id_type=pl.DeviceIdType.MESH
        )
    words = vis_ref[...] * (BASE_SPAN * FRACS) + base_ref[...] * FRACS + frac_ref[...]
    for part in range(slots // LANES):
        meta_own[part] = words[:, part * LANES : (part + 1) * LANES]
    meta_all[0] = meta_own[...]
    elem_all[me, 0:CLUSTERS] = gain_ref[...]
    elem_all[me, CLUSTERS : 2 * CLUSTERS] = (tap_ref[...] & (TAP_SPAN - 1)).astype(F32)
    pl.semaphore_wait(barrier, n - 1)

    def remote(src, dst, send, recv, target):
        return pltpu.make_async_remote_copy(
            src_ref=src, dst_ref=dst, send_sem=send, recv_sem=recv,
            device_id={"link": target}, device_id_type=pl.DeviceIdType.MESH,
        )

    metas = [
        remote(meta_own, meta_all.at[q], meta_send.at[q], meta_recv.at[q],
               flip(own_set, q) * per_set + place)
        for q in range(1, sets)
    ]
    for copy in metas:
        copy.start()
    own_copy = remote(ray_ref, rays.at[1], fwd_send.at[0], fwd_recv.at[0], sibling)
    own_copy.start()
    far = [
        remote(ray_ref, rays.at[2 * k], ray_send.at[k], ray_recv.at[k],
               own_set * per_set + flip(chip, k) * 2 + core)
        for k in range(1, chips)
    ]
    for copy in far:
        copy.start()
    elems = [
        remote(elem_all.at[me], elem_all.at[me], elem_send.at[step], elem_recv.at[step],
               (me + step) % n)
        for step in range(1, n)
    ]
    for copy in elems:
        copy.start()

    def expand(q):
        def body(user, carry):
            for part in range(slots // LANES):
                row = meta_all[q, part, pl.ds(user, 1), :]
                ids = lax.shift_right_logical(row, jnp.int32(10))
                square = jnp.transpose(jnp.broadcast_to(ids, (LANES, LANES)))
                at = pl.multiple_of((q * users + user) * slots + part * LANES, LANES)
                id_cols[pl.ds(at, LANES), :] = square
            return carry

        lax.fori_loop(0, users, body, 0)

    def prepare(k):
        for other in range(2):
            block = ray_ref[...] if k == 0 and other == 0 else rays[2 * k + other]
            high, low = split(block)
            ray_split[other * owned : (other + 1) * owned, 0:LANES] = high
            ray_split[other * owned : (other + 1) * owned, LANES : 2 * LANES] = low

    def pick(k, first_chunk, last_chunk):
        first = own_set * per_set + flip(chip, k) * 2
        bases = ((first + core) * owned, (first + 1 - core) * owned)

        def body(chunk, carry):
            at = pl.multiple_of(chunk * slots, slots)
            ids = id_cols[pl.ds(at, slots), :]
            lane = lax.broadcasted_iota(jnp.int32, (slots, LANES), 1)
            hot = []
            for start in bases:
                shifted = ids - (lane + start)
                for tile in range(owned // LANES):
                    hot.append(jnp.where(shifted == tile * LANES, F32(1), F32(0)).astype(BF16))
            found = jnp.dot(
                jnp.concatenate(hot, axis=1), ray_split[...], preferred_element_type=F32
            )
            if k == 0:
                picked[pl.ds(at, slots), :] = found
            else:
                picked[pl.ds(at, slots), :] += found
            return carry

        lax.fori_loop(first_chunk, last_chunk, body, 0)

    expand(0)
    own_copy.wait()
    prepare(0)
    pick(0, 0, users)
    for q in range(1, sets):
        metas[q - 1].wait()
        expand(q)
    if sets > 1:
        pick(0, users, sets * users)
    forwards = []
    for k in range(1, chips):
        far[k - 1].wait_recv()
        copy = remote(rays.at[2 * k], rays.at[2 * k + 1], fwd_send.at[k], fwd_recv.at[k], sibling)
        copy.start()
        forwards.append(copy)
        copy.wait_recv()
        prepare(k)
        pick(k, 0, sets * users)

    def zones_of(q):
        def body(user, carry):
            row = jnp.concatenate(
                [meta_all[q, part, pl.ds(user, 1), :] for part in range(slots // LANES)], axis=1
            )
            frac = (row & (FRACS - 1)).astype(F32) * F32(1.0 / FRACS)
            base = lax.shift_right_logical(row, jnp.int32(4)) & (BASE_SPAN - 1)
            cluster = lax.shift_right_logical(row, jnp.int32(10)) & (CLUSTERS - 1)
            weights = (
                -frac * (frac - 1.0) * (frac - 2.0) / 6.0,
                (frac + 1.0) * (frac - 1.0) * (frac - 2.0) / 2.0,
                -(frac + 1.0) * frac * (frac - 2.0) / 2.0,
                (frac + 1.0) * frac * (frac - 1.0) / 6.0,
            )
            offset = lax.broadcasted_iota(jnp.int32, (PLACE_ROWS, slots), 0) - (
                base * CLUSTERS + cluster
            )
            matrix = jnp.zeros((PLACE_ROWS, slots), F32)
            for tap in range(TAPS):
                matrix = jnp.where(offset == tap * CLUSTERS, weights[tap], matrix)
            high, low = split(matrix)
            at = pl.multiple_of((q * users + user) * slots, slots)
            rows = picked[pl.ds(at, slots), :].astype(BF16)
            main = jnp.dot(high, rows, preferred_element_type=F32)
            rest = jnp.dot(low, rows[:, 0:LANES], preferred_element_type=F32)
            stacked = main[:, 0:LANES] + main[:, LANES : 2 * LANES] + rest
            lane = lax.broadcasted_iota(jnp.int32, (CLUSTERS, LANES), 1)
            early = stacked[0:CLUSTERS]
            late = jnp.zeros((CLUSTERS, LANES), F32)
            for delay in range(1, BASE_SPAN + TAPS - 1):
                turned = pltpu.roll(
                    stacked[delay * CLUSTERS : (delay + 1) * CLUSTERS], delay, axis=1
                )
                early = early + jnp.where(lane >= delay, turned, F32(0))
                late = late + jnp.where(lane < delay, turned, F32(0))
            out = pl.multiple_of(user * CLUSTERS, CLUSTERS)
            zone_part[q, pl.ds(out, CLUSTERS), 0:LANES] = early
            zone_part[q, pl.ds(out, CLUSTERS), LANES : 2 * LANES] = late
            return carry

        lax.fori_loop(0, users, body, 0)

    backs = []
    for q in range(1, sets):
        zones_of(q)
        copy = remote(zone_part.at[q], zone_got.at[q], zone_send.at[q], zone_recv.at[q],
                      flip(own_set, q) * per_set + place)
        copy.start()
        backs.append(copy)
    zones_of(0)
    for copy in elems:
        copy.wait_recv()
    elem_ref[...] = jnp.concatenate([elem_all[owner] for owner in range(n)], axis=1)
    total = zone_part[0]
    for q in range(1, sets):
        backs[q - 1].wait()
        total = total + zone_got[q]
    zone_ref[...] = total
    for copy in elems:
        copy.wait_send()
    for copy in far:
        copy.wait_send()
    for copy in forwards:
        copy.wait_send()


def element_kernel(zone_ref, elem_ref, out_ref, windows):
    users = zone_ref.shape[0] // CLUSTERS
    depth = TAP_SPAN * CLUSTERS

    @pl.when(pl.program_id(0) == 0)
    def _():
        lane = lax.broadcasted_iota(jnp.int32, (CLUSTERS, LANES), 1)
        for user in range(users):
            early = zone_ref[user * CLUSTERS : (user + 1) * CLUSTERS, 0:LANES]
            late = zone_ref[user * CLUSTERS : (user + 1) * CLUSTERS, LANES : 2 * LANES]
            tiles = []
            for delay in range(TAP_SPAN):
                ahead = TAP_SPAN - delay
                tiles.append(pltpu.roll(jnp.where(lane >= ahead, early, late), LANES - ahead, axis=1))
            high, low = split(jnp.concatenate(tiles, axis=0))
            at = user * LANES
            windows[0:depth, at : at + LANES] = high
            windows[depth : 2 * depth, at : at + LANES] = high
            windows[2 * depth : 3 * depth, at : at + LANES] = low

    gain = elem_ref[0:CLUSTERS]
    tap = elem_ref[CLUSTERS : 2 * CLUSTERS]
    table = jnp.concatenate(
        [jnp.where(tap == F32(delay), gain, F32(0)) for delay in range(TAP_SPAN)], axis=0
    )
    high, low = split(jnp.transpose(table))
    result = jnp.dot(
        jnp.concatenate([high, low, high], axis=1), windows[...], preferred_element_type=F32
    )
    for user in range(users):
        out_ref[user] = result[:, user * LANES : (user + 1) * LANES]


def on_device(n, ray_rows, visible, base_tap, frac_index, elem_tap, elem_gain):
    users, slots = visible.shape
    owned = ray_rows.shape[0]
    per_dev = elem_tap.shape[1]
    elements = n * per_dev
    sets = SETS
    per_set = n // sets
    chips = per_set // 2
    dma = pltpu.SemaphoreType.DMA
    vmem = pl.BlockSpec(memory_space=pltpu.VMEM)
    zones, elem = pl.pallas_call(
        functools.partial(zone_kernel, n, sets),
        out_shape=(
            jax.ShapeDtypeStruct((users * CLUSTERS, 2 * LANES), F32),
            jax.ShapeDtypeStruct((2 * CLUSTERS, elements), F32),
        ),
        in_specs=[vmem] * 6,
        out_specs=(vmem, vmem),
        scratch_shapes=[
            pltpu.VMEM((per_set, owned, LANES), F32),
            pltpu.VMEM((n, 2 * CLUSTERS, per_dev), F32),
            pltpu.VMEM((slots // LANES, users, LANES), jnp.int32),
            pltpu.VMEM((sets, slots // LANES, users, LANES), jnp.int32),
            pltpu.VMEM((sets * users * slots, LANES), jnp.int32),
            pltpu.VMEM((2 * owned, 2 * LANES), BF16),
            pltpu.VMEM((sets * users * slots, 2 * LANES), F32),
            pltpu.VMEM((sets, users * CLUSTERS, 2 * LANES), F32),
            pltpu.VMEM((sets, users * CLUSTERS, 2 * LANES), F32),
            dma((chips,)), dma((chips,)), dma((chips,)), dma((chips,)),
            dma((sets,)), dma((sets,)), dma((n,)), dma((n,)), dma((sets,)), dma((sets,)),
        ],
        compiler_params=pltpu.CompilerParams(
            collective_id=0, has_side_effects=True, vmem_limit_bytes=48 * 2**20
        ),
        name="zones",
    )(ray_rows, visible, base_tap, frac_index, elem_tap, elem_gain)

    block = 256
    return pl.pallas_call(
        element_kernel,
        grid=(elements // block,),
        out_shape=jax.ShapeDtypeStruct((users, elements, SAMPLES), F32),
        in_specs=[
            pl.BlockSpec((users * CLUSTERS, 2 * LANES), lambda step: (0, 0)),
            pl.BlockSpec((2 * CLUSTERS, block), lambda step: (0, step)),
        ],
        out_specs=pl.BlockSpec((users, block, SAMPLES), lambda step: (0, step, 0)),
        scratch_shapes=[pltpu.VMEM((3 * TAP_SPAN * CLUSTERS, users * LANES), BF16)],
        compiler_params=pltpu.CompilerParams(vmem_limit_bytes=48 * 2**20),
        name="elements",
    )(zones, elem)


def solution(mesh):
    in_specs = (
        P(("group", "link"), None),
        P(("group", "link"), None),
        P(("group", "link"), None),
        P(("group", "link"), None),
        P(None, "link"),
        P(None, "link"),
    )
    out_specs = P(("group", "link"), None, None)
    return jax.shard_map(
        functools.partial(on_device, mesh.shape["link"]),
        mesh=mesh, in_specs=in_specs, out_specs=out_specs, check_vma=False,
    )
```

```python
import functools

import jax
import jax.numpy as jnp
from jax import lax
from jax.experimental import pallas as pl
from jax.experimental.pallas import tpu as pltpu
from jax.sharding import PartitionSpec as P

SAMPLES = 128
TAP_SPAN = 32
BASE_SPAN = 64
FRACS = 16
CLUSTERS = 8
LANES = 128
TAPS = 4
PLACE_ROWS = -(-(BASE_SPAN + TAPS - 1) * CLUSTERS // 16) * 16
PICK_ROWS = 1024
PACK = 128 // TAP_SPAN
SETS = 2

F32 = jnp.float32
BF16 = jnp.bfloat16


def flip(value, mask, limit):
    result = value
    bit = 1
    while bit < limit:
        result = result + bit * ((mask // bit) % 2) * (1 - 2 * ((value // bit) % 2))
        bit *= 2
    return result


def split(value):
    high = value.astype(BF16)
    return high, (value - high.astype(F32)).astype(BF16)


def zone_kernel(
    n, sets,
    ray_ref, vis_hbm, base_hbm, frac_hbm, tap_hbm, gain_hbm,
    zone_ref, table_ref,
    vis_ref, base_ref, frac_ref, tap_ref, gain_ref,
    rays, elem_all, meta_own, meta_all, id_cols, ray_split, picked, places, table, zone_part,
    zone_got, load_sem, table_sem, ray_send, ray_recv, fwd_send, fwd_recv, meta_send, meta_recv, elem_send, elem_recv,
    zone_send, zone_recv,
):
    per_set = n // sets
    chips = per_set // 2
    me = lax.axis_index("link")
    own_set = me // per_set
    place = me % per_set
    chip = place // 2
    core = place % 2
    sibling = me + 1 - 2 * core
    users, slots = vis_ref.shape
    owned = ray_ref.shape[0]
    per_dev = tap_ref.shape[1]

    loads = [
        pltpu.make_async_copy(src, dst, load_sem.at[i])
        for i, (src, dst) in enumerate((
            (vis_hbm, vis_ref), (base_hbm, base_ref), (frac_hbm, frac_ref),
            (tap_hbm, tap_ref), (gain_hbm, gain_ref), (ray_ref, rays.at[0]),
        ))
    ]
    for load in loads:
        load.start()
    barrier = pltpu.get_barrier_semaphore()
    for step in range(1, n):
        pl.semaphore_signal(
            barrier, inc=1, device_id={"link": (me + step) % n}, device_id_type=pl.DeviceIdType.MESH
        )
    for load in loads[:-1]:
        load.wait()
    words = vis_ref[...] * (BASE_SPAN * FRACS) + base_ref[...] * FRACS + frac_ref[...]
    for part in range(slots // LANES):
        meta_own[part] = words[:, part * LANES : (part + 1) * LANES]
    meta_all[0] = meta_own[...]
    elem_all[me, 0:CLUSTERS] = gain_ref[...]
    elem_all[me, CLUSTERS : 2 * CLUSTERS] = (tap_ref[...] & (TAP_SPAN - 1)).astype(F32)
    picked[...] = jnp.zeros_like(picked)
    pl.semaphore_wait(barrier, n - 1)

    def remote(src, dst, send, recv, target):
        return pltpu.make_async_remote_copy(
            src_ref=src, dst_ref=dst, send_sem=send, recv_sem=recv,
            device_id={"link": target}, device_id_type=pl.DeviceIdType.MESH,
        )

    metas = [
        remote(meta_own, meta_all.at[q], meta_send.at[q], meta_recv.at[q],
               flip(own_set, q, sets) * per_set + place)
        for q in range(1, sets)
    ]
    for copy in metas:
        copy.start()
    elems = [
        remote(elem_all.at[me], elem_all.at[me], elem_send.at[step], elem_recv.at[step],
               (me + step) % n)
        for step in range(1, n)
    ]
    for copy in elems:
        copy.start()

    own_copy = remote(ray_ref, rays.at[1], fwd_send.at[0], fwd_recv.at[0], sibling)
    own_copy.start()

    def far_copy(k):
        return remote(ray_ref, rays.at[2 * k], ray_send.at[k], ray_recv.at[k],
                      own_set * per_set + flip(chip, k, chips) * 2 + core)

    def forward_copy(k):
        return remote(rays.at[2 * k], rays.at[2 * k + 1], fwd_send.at[k], fwd_recv.at[k], sibling)

    far = [far_copy(k) for k in range(1, chips)]
    for copy in far:
        copy.start()
    def expand():
        def body(index, carry):
            q, user = index // users, index % users
            for part in range(slots // LANES):
                row = meta_all[q, part, pl.ds(user, 1), :]
                ids = lax.shift_right_logical(row, jnp.int32(10))
                square = jnp.transpose(jnp.broadcast_to(ids, (LANES, LANES)))
                at = pl.multiple_of(index * slots + part * LANES, LANES)
                id_cols[pl.ds(at, LANES), :] = square
            return carry

        lax.fori_loop(0, sets * users, body, 0)

    def prepare(k):
        for other in range(2):
            high, low = split(rays[2 * k + other])
            ray_split[other * owned : (other + 1) * owned, 0:LANES] = high
            ray_split[other * owned : (other + 1) * owned, LANES : 2 * LANES] = low

    def pick(k):
        first = own_set * per_set + flip(chip, k, chips) * 2
        bases = ((first + core) * owned, (first + 1 - core) * owned)

        def body(chunk, carry):
            at = pl.multiple_of(chunk * PICK_ROWS, PICK_ROWS)
            ids = id_cols[pl.ds(at, PICK_ROWS), :]
            lane = lax.broadcasted_iota(jnp.int32, (PICK_ROWS, LANES), 1)
            hot = []
            for start in bases:
                shifted = ids - (lane + start)
                for tile in range(owned // LANES):
                    hot.append(jnp.where(shifted == tile * LANES, F32(1), F32(0)).astype(BF16))
            found = jnp.dot(
                jnp.concatenate(hot, axis=1), ray_split[...], preferred_element_type=F32
            )
            picked[pl.ds(at, PICK_ROWS), :] += found
            return carry

        lax.fori_loop(0, sets * users * slots // PICK_ROWS, body, 0)

    def weigh():
        def body(index, carry):
            q, user = index // users, index % users
            row = jnp.concatenate(
                [meta_all[q, part, pl.ds(user, 1), :] for part in range(slots // LANES)], axis=1
            )
            frac = (row & (FRACS - 1)).astype(F32) * F32(1.0 / FRACS)
            base = lax.shift_right_logical(row, jnp.int32(4)) & (BASE_SPAN - 1)
            cluster = lax.shift_right_logical(row, jnp.int32(10)) & (CLUSTERS - 1)
            weights = (
                -frac * (frac - 1.0) * (frac - 2.0) / 6.0,
                (frac + 1.0) * (frac - 1.0) * (frac - 2.0) / 2.0,
                -(frac + 1.0) * frac * (frac - 2.0) / 2.0,
                (frac + 1.0) * frac * (frac - 1.0) / 6.0,
            )
            offset = lax.broadcasted_iota(jnp.int32, (PLACE_ROWS, slots), 0) - (
                base * CLUSTERS + cluster
            )
            matrix = jnp.zeros((PLACE_ROWS, slots), F32)
            for tap in range(TAPS):
                matrix = jnp.where(offset == tap * CLUSTERS, weights[tap], matrix)
            high, low = split(matrix)
            places[index, 0] = high
            places[index, 1] = low
            return carry

        lax.fori_loop(0, sets * users, body, 0)

    def tabulate():
        owners = LANES // per_dev

        def body(tile, carry):
            both = jnp.concatenate(
                [elem_all[tile * owners + inner] for inner in range(owners)], axis=1
            )
            gain = both[0:CLUSTERS]
            tap = both[CLUSTERS : 2 * CLUSTERS]
            wide = jnp.concatenate(
                [jnp.where(tap == F32(delay), gain, F32(0)) for delay in range(TAP_SPAN)], axis=0
            )
            high, low = split(jnp.transpose(wide))
            at = pl.multiple_of(tile * LANES, LANES)
            depth = TAP_SPAN * CLUSTERS
            table[pl.ds(at, LANES), 0:depth] = high
            table[pl.ds(at, LANES), depth : 2 * depth] = low
            return carry

        lax.fori_loop(0, n // owners, body, 0)

    for copy in metas:
        copy.wait()
    expand()
    loads[-1].wait()
    own_copy.wait()
    store = pltpu.make_async_copy(table, table_ref, table_sem)

    def take(k, carry):
        @pl.when(k > 0)
        def _():
            far_copy(k).wait_recv()
            forward = forward_copy(k)
            forward.start()
            forward.wait_recv()

        prepare(k)
        pick(k)

        @pl.when(k == 0)
        def _():
            weigh()

        @pl.when(k == max(chips - 2, 0))
        def _():
            for copy in elems:
                copy.wait_recv()
            tabulate()
            store.start()

        return carry

    lax.fori_loop(0, chips, take, 0)

    def zones_of(q, pack):
        lane = lax.broadcasted_iota(jnp.int32, (CLUSTERS, LANES), 1)
        shared = jnp.zeros((CLUSTERS, LANES), F32)
        for inner in range(PACK):
            index = q * users + pack * PACK + inner
            rows = picked[pl.ds(pl.multiple_of(index * slots, slots), slots), :].astype(BF16)
            main = jnp.dot(places[index, 0], rows, preferred_element_type=F32)
            rest = jnp.dot(places[index, 1], rows[:, 0:LANES], preferred_element_type=F32)
            stacked = main[:, 0:LANES] + main[:, LANES : 2 * LANES] + rest
            early = stacked[0:CLUSTERS]
            late = jnp.zeros((CLUSTERS, LANES), F32)
            for delay in range(1, BASE_SPAN + TAPS - 1):
                turned = pltpu.roll(
                    stacked[delay * CLUSTERS : (delay + 1) * CLUSTERS], delay, axis=1
                )
                early = early + jnp.where(lane >= delay, turned, F32(0))
                late = late + jnp.where(lane < delay, turned, F32(0))
            zone_part[q, pack, inner * CLUSTERS : (inner + 1) * CLUSTERS, :] = early
            mine = late if inner == 0 else pltpu.roll(late, inner * TAP_SPAN, axis=1)
            inside = (lane >= inner * TAP_SPAN) & (lane < (inner + 1) * TAP_SPAN)
            shared = jnp.where(inside, mine, shared)
        zone_part[q, pack, PACK * CLUSTERS : (PACK + 1) * CLUSTERS, :] = shared

    packs = users // PACK

    def zone_copy(q, pack):
        return remote(zone_part.at[q, pack], zone_got.at[q, pack], zone_send.at[q, pack],
                      zone_recv.at[q, pack], flip(own_set, q, sets) * per_set + place)

    def make(index, carry):
        q, pack = sets - 1 - index // packs, index % packs
        zones_of(q, pack)

        @pl.when(q > 0)
        def _():
            zone_copy(q, pack).start()

        return carry

    lax.fori_loop(0, sets * packs, make, 0)
    for q in range(1, sets):
        for pack in range(packs):
            zone_copy(q, pack).wait()
    total = zone_part[0]
    for q in range(1, sets):
        total = total + zone_got[q]
    zone_ref[...] = total
    store.wait()
    for copy in elems:
        copy.wait_send()
    for k in range(1, chips):
        far_copy(k).wait_send()
        forward_copy(k).wait_send()


def element_kernel(zone_ref, table_ref, out_ref, windows):
    users = zone_ref.shape[0] * PACK
    depth = TAP_SPAN * CLUSTERS

    @pl.when(pl.program_id(0) == 0)
    def _():
        lane = lax.broadcasted_iota(jnp.int32, (CLUSTERS, LANES), 1)
        for user in range(users):
            pack, inner = user // PACK, user % PACK
            early = zone_ref[pack, inner * CLUSTERS : (inner + 1) * CLUSTERS, :]
            late = zone_ref[pack, PACK * CLUSTERS : (PACK + 1) * CLUSTERS, :]
            if inner:
                late = pltpu.roll(late, LANES - inner * TAP_SPAN, axis=1)
            tiles = []
            for delay in range(TAP_SPAN):
                ahead = TAP_SPAN - delay
                tiles.append(pltpu.roll(jnp.where(lane >= ahead, early, late), LANES - ahead, axis=1))
            high, low = split(jnp.concatenate(tiles, axis=0))
            at = user * LANES
            windows[0:depth, at : at + LANES] = high
            windows[depth : 2 * depth, at : at + LANES] = high
            windows[2 * depth : 3 * depth, at : at + LANES] = low

    both = table_ref[...]
    result = jnp.dot(
        jnp.concatenate([both, both[:, 0:depth]], axis=1), windows[...], preferred_element_type=F32
    )
    for user in range(users):
        out_ref[user] = result[:, user * LANES : (user + 1) * LANES]


def on_device(n, ray_rows, visible, base_tap, frac_index, elem_tap, elem_gain):
    users, slots = visible.shape
    owned = ray_rows.shape[0]
    per_dev = elem_tap.shape[1]
    elements = n * per_dev
    sets = SETS
    per_set = n // sets
    chips = per_set // 2
    dma = pltpu.SemaphoreType.DMA
    vmem = pl.BlockSpec(memory_space=pltpu.VMEM)
    hbm = pl.BlockSpec(memory_space=pl.ANY)
    packs = users // PACK
    depth = TAP_SPAN * CLUSTERS
    packed = ((PACK + 1) * CLUSTERS, LANES)
    zones, table = pl.pallas_call(
        functools.partial(zone_kernel, n, sets),
        out_shape=(
            jax.ShapeDtypeStruct((packs,) + packed, F32),
            jax.ShapeDtypeStruct((elements, 2 * depth), BF16),
        ),
        in_specs=[hbm] * 6,
        out_specs=(vmem, hbm),
        scratch_shapes=[
            pltpu.VMEM((users, slots), jnp.int32),
            pltpu.VMEM((users, slots), jnp.int32),
            pltpu.VMEM((users, slots), jnp.int32),
            pltpu.VMEM((CLUSTERS, per_dev), jnp.int32),
            pltpu.VMEM((CLUSTERS, per_dev), F32),
            pltpu.VMEM((per_set, owned, LANES), F32),
            pltpu.VMEM((n, 2 * CLUSTERS, per_dev), F32),
            pltpu.VMEM((slots // LANES, users, LANES), jnp.int32),
            pltpu.VMEM((sets, slots // LANES, users, LANES), jnp.int32),
            pltpu.VMEM((sets * users * slots, LANES), jnp.int32),
            pltpu.VMEM((2 * owned, 2 * LANES), BF16),
            pltpu.VMEM((sets * users * slots, 2 * LANES), F32),
            pltpu.VMEM((sets * users, 2, PLACE_ROWS, slots), BF16),
            pltpu.VMEM((elements, 2 * depth), BF16),
            pltpu.VMEM((sets, packs) + packed, F32),
            pltpu.VMEM((sets, packs) + packed, F32),
            dma((6,)), dma,
            dma((chips,)), dma((chips,)), dma((chips,)), dma((chips,)),
            dma((sets,)), dma((sets,)), dma((n,)), dma((n,)),
            dma((sets, packs)), dma((sets, packs)),
        ],
        compiler_params=pltpu.CompilerParams(
            collective_id=0, has_side_effects=True, vmem_limit_bytes=56 * 2**20
        ),
        name="zones",
    )(ray_rows, visible, base_tap, frac_index, elem_tap, elem_gain)

    block = 512
    return pl.pallas_call(
        element_kernel,
        grid=(elements // block,),
        out_shape=jax.ShapeDtypeStruct((users, elements, SAMPLES), F32),
        in_specs=[
            pl.BlockSpec((packs,) + packed, lambda step: (0, 0, 0)),
            pl.BlockSpec((block, 2 * depth), lambda step: (step, 0)),
        ],
        out_specs=pl.BlockSpec((users, block, SAMPLES), lambda step: (0, step, 0)),
        scratch_shapes=[pltpu.VMEM((3 * depth, users * LANES), BF16)],
        compiler_params=pltpu.CompilerParams(vmem_limit_bytes=63 * 2**20),
        name="elements",
    )(zones, table)


def solution(mesh):
    in_specs = (
        P(("group", "link"), None),
        P(("group", "link"), None),
        P(("group", "link"), None),
        P(("group", "link"), None),
        P(None, "link"),
        P(None, "link"),
    )
    out_specs = P(("group", "link"), None, None)
    return jax.shard_map(
        functools.partial(on_device, mesh.shape["link"]),
        mesh=mesh, in_specs=in_specs, out_specs=out_specs, check_vma=False,
    )
```

```python
import functools

import jax
import jax.numpy as jnp
from jax import lax
from jax.experimental import pallas as pl
from jax.experimental.pallas import tpu as pltpu
from jax.sharding import PartitionSpec as P

SAMPLES = 128
TAP_SPAN = 32
BASE_SPAN = 64
FRACS = 16
CLUSTERS = 8
LANES = 128
TAPS = 4
PLACE_ROWS = -(-(BASE_SPAN + TAPS - 1) * CLUSTERS // 16) * 16
PICK_ROWS = 2048
PACK = 128 // TAP_SPAN
SETS = 2

F32 = jnp.float32
BF16 = jnp.bfloat16


def flip(value, mask, limit):
    result = value
    bit = 1
    while bit < limit:
        result = result + bit * ((mask // bit) % 2) * (1 - 2 * ((value // bit) % 2))
        bit *= 2
    return result


def split(value):
    high = value.astype(BF16)
    return high, (value - high.astype(F32)).astype(BF16)


def zone_kernel(
    n, sets,
    ray_ref, vis_hbm, base_hbm, frac_hbm, tap_hbm, gain_hbm,
    zone_ref, table_ref,
    vis_ref, base_ref, frac_ref, tap_ref, gain_ref,
    rays, elem_all, meta_own, meta_all, id_cols, ray_split, picked, places, table, zone_part,
    zone_got, load_sem, table_sem, ray_send, ray_recv, fwd_send, fwd_recv, meta_send, meta_recv, elem_send, elem_recv,
    zone_send, zone_recv,
):
    per_set = n // sets
    chips = per_set // 2
    me = lax.axis_index("link")
    own_set = me // per_set
    place = me % per_set
    chip = place // 2
    core = place % 2
    sibling = me + 1 - 2 * core
    users, slots = vis_ref.shape
    owned = ray_ref.shape[0]
    per_dev = tap_ref.shape[1]

    loads = [
        pltpu.make_async_copy(src, dst, load_sem.at[i])
        for i, (src, dst) in enumerate((
            (vis_hbm, vis_ref), (base_hbm, base_ref), (frac_hbm, frac_ref),
            (tap_hbm, tap_ref), (gain_hbm, gain_ref), (ray_ref, rays.at[0]),
        ))
    ]
    for load in loads:
        load.start()
    barrier = pltpu.get_barrier_semaphore()
    for step in range(1, n):
        pl.semaphore_signal(
            barrier, inc=1, device_id={"link": (me + step) % n}, device_id_type=pl.DeviceIdType.MESH
        )
    for load in loads[:-1]:
        load.wait()
    words = vis_ref[...] * (BASE_SPAN * FRACS) + base_ref[...] * FRACS + frac_ref[...]
    for part in range(slots // LANES):
        meta_own[part] = words[:, part * LANES : (part + 1) * LANES]
    meta_all[0] = meta_own[...]
    elem_all[me, 0:CLUSTERS] = gain_ref[...]
    elem_all[me, CLUSTERS : 2 * CLUSTERS] = (tap_ref[...] & (TAP_SPAN - 1)).astype(F32)
    def expand(first, last):
        def body(index, carry):
            q, user = index // users, index % users
            for part in range(slots // LANES):
                row = meta_all[q, part, pl.ds(user, 1), :]
                ids = lax.shift_right_logical(row, jnp.int32(10))
                square = jnp.transpose(jnp.broadcast_to(ids, (LANES, LANES)))
                at = pl.multiple_of(index * slots + part * LANES, LANES)
                id_cols[pl.ds(at, LANES), :] = square
            return carry

        lax.fori_loop(first, last, body, 0)

    def weigh(first, last):
        def body(index, carry):
            q, user = index // users, index % users
            row = jnp.concatenate(
                [meta_all[q, part, pl.ds(user, 1), :] for part in range(slots // LANES)], axis=1
            )
            frac = (row & (FRACS - 1)).astype(F32) * F32(1.0 / FRACS)
            base = lax.shift_right_logical(row, jnp.int32(4)) & (BASE_SPAN - 1)
            cluster = lax.shift_right_logical(row, jnp.int32(10)) & (CLUSTERS - 1)
            weights = (
                -frac * (frac - 1.0) * (frac - 2.0) / 6.0,
                (frac + 1.0) * (frac - 1.0) * (frac - 2.0) / 2.0,
                -(frac + 1.0) * frac * (frac - 2.0) / 2.0,
                (frac + 1.0) * frac * (frac - 1.0) / 6.0,
            )
            delays = PLACE_ROWS // CLUSTERS
            offset = lax.broadcasted_iota(jnp.int32, (delays, slots), 0) - base
            matrix = jnp.zeros((delays, slots), F32)
            for tap in range(TAPS):
                matrix = jnp.where(offset == tap, weights[tap], matrix)
            top = matrix.astype(BF16).astype(F32)
            member = lax.broadcasted_iota(jnp.int32, (CLUSTERS, slots), 0) == cluster

            def by_cluster(values):
                return jnp.concatenate(
                    [jnp.where(member, values[at : at + 1], F32(0)) for at in range(delays)], axis=0
                ).astype(BF16)

            high, low = by_cluster(top), by_cluster(matrix - top)
            places[index, 0] = high
            places[index, 1] = low
            return carry

        lax.fori_loop(first, last, body, 0)

    picked[...] = jnp.zeros_like(picked)
    expand(0, users)
    pl.semaphore_wait(barrier, n - 1)

    def remote(src, dst, send, recv, target):
        return pltpu.make_async_remote_copy(
            src_ref=src, dst_ref=dst, send_sem=send, recv_sem=recv,
            device_id={"link": target}, device_id_type=pl.DeviceIdType.MESH,
        )

    metas = [
        remote(meta_own, meta_all.at[q], meta_send.at[q], meta_recv.at[q],
               flip(own_set, q, sets) * per_set + place)
        for q in range(1, sets)
    ]
    for copy in metas:
        copy.start()
    elems = [
        remote(elem_all.at[me], elem_all.at[me], elem_send.at[step], elem_recv.at[step],
               (me + step) % n)
        for step in range(1, n)
    ]
    for copy in elems:
        copy.start()

    own_copy = remote(ray_ref, rays.at[1], fwd_send.at[0], fwd_recv.at[0], sibling)
    own_copy.start()

    def far_copy(k):
        return remote(ray_ref, rays.at[2 * k], ray_send.at[k], ray_recv.at[k],
                      own_set * per_set + flip(chip, k, chips) * 2 + core)

    def forward_copy(k):
        return remote(rays.at[2 * k], rays.at[2 * k + 1], fwd_send.at[k], fwd_recv.at[k], sibling)

    far = [far_copy(k) for k in range(1, chips)]
    for copy in far:
        copy.start()
    def prepare(k):
        for other in range(2):
            high, low = split(rays[2 * k + other])
            ray_split[other * owned : (other + 1) * owned, 0:LANES] = high
            ray_split[other * owned : (other + 1) * owned, LANES : 2 * LANES] = low

    def pick(k):
        first = own_set * per_set + flip(chip, k, chips) * 2
        bases = ((first + core) * owned, (first + 1 - core) * owned)

        def body(chunk, carry):
            at = pl.multiple_of(chunk * PICK_ROWS, PICK_ROWS)
            ids = id_cols[pl.ds(at, PICK_ROWS), :]
            lane = lax.broadcasted_iota(jnp.int32, (PICK_ROWS, LANES), 1)
            hot = []
            for start in bases:
                shifted = ids - (lane + start)
                for tile in range(owned // LANES):
                    hot.append(jnp.where(shifted == tile * LANES, F32(1), F32(0)).astype(BF16))
            found = jnp.dot(
                jnp.concatenate(hot, axis=1), ray_split[...], preferred_element_type=F32
            )
            picked[pl.ds(at, PICK_ROWS), :] += found
            return carry

        lax.fori_loop(0, sets * users * slots // PICK_ROWS, body, 0)

    def tabulate():
        owners = LANES // per_dev

        def body(tile, carry):
            both = jnp.concatenate(
                [elem_all[tile * owners + inner] for inner in range(owners)], axis=1
            )
            gain = both[0:CLUSTERS]
            tap = both[CLUSTERS : 2 * CLUSTERS]
            wide = jnp.concatenate(
                [jnp.where(tap == F32(delay), gain, F32(0)) for delay in range(TAP_SPAN)], axis=0
            )
            high, low = split(jnp.transpose(wide))
            at = pl.multiple_of(tile * LANES, LANES)
            depth = TAP_SPAN * CLUSTERS
            table[pl.ds(at, LANES), 0:depth] = high
            table[pl.ds(at, LANES), depth : 2 * depth] = low
            return carry

        lax.fori_loop(0, n // owners, body, 0)

    weigh(0, users)
    for copy in metas:
        copy.wait()
    expand(users, sets * users)
    loads[-1].wait()
    own_copy.wait()
    store = pltpu.make_async_copy(table, table_ref, table_sem)

    def take(k, carry):
        @pl.when(k > 0)
        def _():
            far_copy(k).wait_recv()
            forward = forward_copy(k)
            forward.start()
            forward.wait_recv()

        prepare(k)
        pick(k)

        @pl.when(k == 0)
        def _():
            weigh(users, sets * users)

        @pl.when(k == max(chips - 2, 0))
        def _():
            for copy in elems:
                copy.wait_recv()
            tabulate()
            store.start()

        return carry

    lax.fori_loop(0, chips, take, 0)

    def zones_of(q, pack):
        lane = lax.broadcasted_iota(jnp.int32, (CLUSTERS, LANES), 1)
        shared = jnp.zeros((CLUSTERS, LANES), F32)
        for inner in range(PACK):
            index = q * users + pack * PACK + inner
            rows = picked[pl.ds(pl.multiple_of(index * slots, slots), slots), :].astype(BF16)
            main = jnp.dot(places[index, 0], rows, preferred_element_type=F32)
            rest = jnp.dot(places[index, 1], rows[:, 0:LANES], preferred_element_type=F32)
            stacked = main[:, 0:LANES] + main[:, LANES : 2 * LANES] + rest
            early = stacked[0:CLUSTERS]
            late = jnp.zeros((CLUSTERS, LANES), F32)
            for delay in range(1, BASE_SPAN + TAPS - 1):
                turned = pltpu.roll(
                    stacked[delay * CLUSTERS : (delay + 1) * CLUSTERS], delay, axis=1
                )
                early = early + jnp.where(lane >= delay, turned, F32(0))
                late = late + jnp.where(lane < delay, turned, F32(0))
            zone_part[q, pack, inner * CLUSTERS : (inner + 1) * CLUSTERS, :] = early
            mine = late if inner == 0 else pltpu.roll(late, inner * TAP_SPAN, axis=1)
            inside = (lane >= inner * TAP_SPAN) & (lane < (inner + 1) * TAP_SPAN)
            shared = jnp.where(inside, mine, shared)
        zone_part[q, pack, PACK * CLUSTERS : (PACK + 1) * CLUSTERS, :] = shared

    packs = users // PACK

    def zone_copy(q, pack):
        return remote(zone_part.at[q, pack], zone_got.at[q, pack], zone_send.at[q, pack],
                      zone_recv.at[q, pack], flip(own_set, q, sets) * per_set + place)

    def make(index, carry):
        q, pack = sets - 1 - index // packs, index % packs
        zones_of(q, pack)

        @pl.when(q > 0)
        def _():
            zone_copy(q, pack).start()

        return carry

    lax.fori_loop(0, sets * packs, make, 0)
    for q in range(1, sets):
        for pack in range(packs):
            zone_copy(q, pack).wait()
    total = zone_part[0]
    for q in range(1, sets):
        total = total + zone_got[q]
    zone_ref[...] = total
    store.wait()
    for copy in elems:
        copy.wait_send()
    for k in range(1, chips):
        far_copy(k).wait_send()
        forward_copy(k).wait_send()


def element_kernel(zone_ref, table_ref, out_ref, windows):
    users = zone_ref.shape[0] * PACK
    depth = TAP_SPAN * CLUSTERS

    @pl.when(pl.program_id(0) == 0)
    def _():
        lane = lax.broadcasted_iota(jnp.int32, (CLUSTERS, LANES), 1)
        for user in range(users):
            pack, inner = user // PACK, user % PACK
            early = zone_ref[pack, inner * CLUSTERS : (inner + 1) * CLUSTERS, :]
            late = zone_ref[pack, PACK * CLUSTERS : (PACK + 1) * CLUSTERS, :]
            if inner:
                late = pltpu.roll(late, LANES - inner * TAP_SPAN, axis=1)
            tiles = []
            for delay in range(TAP_SPAN):
                ahead = TAP_SPAN - delay
                tiles.append(pltpu.roll(jnp.where(lane >= ahead, early, late), LANES - ahead, axis=1))
            high, low = split(jnp.concatenate(tiles, axis=0))
            at = user * LANES
            windows[0:depth, at : at + LANES] = high
            windows[depth : 2 * depth, at : at + LANES] = high
            windows[2 * depth : 3 * depth, at : at + LANES] = low

    both = table_ref[...]
    terms = jnp.concatenate([both, both[:, 0:depth]], axis=1)
    for user in range(0, users, 2):
        at = user * LANES
        pair = jnp.dot(terms, windows[:, at : at + 2 * LANES], preferred_element_type=F32)
        out_ref[user] = pair[:, 0:LANES]
        out_ref[user + 1] = pair[:, LANES : 2 * LANES]


def on_device(n, ray_rows, visible, base_tap, frac_index, elem_tap, elem_gain):
    users, slots = visible.shape
    owned = ray_rows.shape[0]
    per_dev = elem_tap.shape[1]
    elements = n * per_dev
    sets = SETS
    per_set = n // sets
    chips = per_set // 2
    dma = pltpu.SemaphoreType.DMA
    vmem = pl.BlockSpec(memory_space=pltpu.VMEM)
    hbm = pl.BlockSpec(memory_space=pl.ANY)
    packs = users // PACK
    depth = TAP_SPAN * CLUSTERS
    packed = ((PACK + 1) * CLUSTERS, LANES)
    zones, table = pl.pallas_call(
        functools.partial(zone_kernel, n, sets),
        out_shape=(
            jax.ShapeDtypeStruct((packs,) + packed, F32),
            jax.ShapeDtypeStruct((elements, 2 * depth), BF16),
        ),
        in_specs=[hbm] * 6,
        out_specs=(vmem, hbm),
        scratch_shapes=[
            pltpu.VMEM((users, slots), jnp.int32),
            pltpu.VMEM((users, slots), jnp.int32),
            pltpu.VMEM((users, slots), jnp.int32),
            pltpu.VMEM((CLUSTERS, per_dev), jnp.int32),
            pltpu.VMEM((CLUSTERS, per_dev), F32),
            pltpu.VMEM((per_set, owned, LANES), F32),
            pltpu.VMEM((n, 2 * CLUSTERS, per_dev), F32),
            pltpu.VMEM((slots // LANES, users, LANES), jnp.int32),
            pltpu.VMEM((sets, slots // LANES, users, LANES), jnp.int32),
            pltpu.VMEM((sets * users * slots, LANES), jnp.int32),
            pltpu.VMEM((2 * owned, 2 * LANES), BF16),
            pltpu.VMEM((sets * users * slots, 2 * LANES), F32),
            pltpu.VMEM((sets * users, 2, PLACE_ROWS, slots), BF16),
            pltpu.VMEM((elements, 2 * depth), BF16),
            pltpu.VMEM((sets, packs) + packed, F32),
            pltpu.VMEM((sets, packs) + packed, F32),
            dma((6,)), dma,
            dma((chips,)), dma((chips,)), dma((chips,)), dma((chips,)),
            dma((sets,)), dma((sets,)), dma((n,)), dma((n,)),
            dma((sets, packs)), dma((sets, packs)),
        ],
        compiler_params=pltpu.CompilerParams(
            collective_id=0, has_side_effects=True, vmem_limit_bytes=56 * 2**20
        ),
        name="zones",
    )(ray_rows, visible, base_tap, frac_index, elem_tap, elem_gain)

    block = 1024
    return pl.pallas_call(
        element_kernel,
        grid=(elements // block,),
        out_shape=jax.ShapeDtypeStruct((users, elements, SAMPLES), F32),
        in_specs=[
            pl.BlockSpec((packs,) + packed, lambda step: (0, 0, 0)),
            pl.BlockSpec((block, 2 * depth), lambda step: (step, 0)),
        ],
        out_specs=pl.BlockSpec((users, block, SAMPLES), lambda step: (0, step, 0)),
        scratch_shapes=[pltpu.VMEM((3 * depth, users * LANES), BF16)],
        compiler_params=pltpu.CompilerParams(vmem_limit_bytes=63 * 2**20),
        name="elements",
    )(zones, table)


def solution(mesh):
    in_specs = (
        P(("group", "link"), None),
        P(("group", "link"), None),
        P(("group", "link"), None),
        P(("group", "link"), None),
        P(None, "link"),
        P(None, "link"),
    )
    out_specs = P(("group", "link"), None, None)
    return jax.shard_map(
        functools.partial(on_device, mesh.shape["link"]),
        mesh=mesh, in_specs=in_specs, out_specs=out_specs, check_vma=False,
    )
```

```python
import functools

import jax
import jax.numpy as jnp
from jax import lax
from jax.experimental import pallas as pl
from jax.experimental.pallas import tpu as pltpu
from jax.sharding import PartitionSpec as P

SAMPLES = 128
TAP_SPAN = 32
BASE_SPAN = 64
FRACS = 16
CLUSTERS = 8
LANES = 128
TAPS = 4
PLACE_ROWS = -(-(BASE_SPAN + TAPS - 1) * CLUSTERS // 16) * 16
PICK_ROWS = 4096
PACK = 128 // TAP_SPAN
SETS = 2

F32 = jnp.float32
BF16 = jnp.bfloat16


def flip(value, mask, limit):
    result = value
    bit = 1
    while bit < limit:
        result = result + bit * ((mask // bit) % 2) * (1 - 2 * ((value // bit) % 2))
        bit *= 2
    return result


def split(value):
    high = value.astype(BF16)
    return high, (value - high.astype(F32)).astype(BF16)


def zone_kernel(
    n, sets,
    ray_ref, vis_hbm, base_hbm, frac_hbm, tap_hbm, gain_hbm,
    zone_ref, table_ref,
    vis_ref, base_ref, frac_ref, tap_ref, gain_ref,
    rays, elem_all, meta_own, meta_all, id_cols, ray_split, picked, places, table, zone_part,
    zone_got, load_sem, table_sem, ray_send, ray_recv, fwd_send, fwd_recv, meta_send, meta_recv, elem_send, elem_recv,
    zone_send, zone_recv,
):
    per_set = n // sets
    chips = per_set // 2
    me = lax.axis_index("link")
    own_set = me // per_set
    place = me % per_set
    chip = place // 2
    core = place % 2
    sibling = me + 1 - 2 * core
    users, slots = vis_ref.shape
    owned = ray_ref.shape[0]
    per_dev = tap_ref.shape[1]

    loads = [
        pltpu.make_async_copy(src, dst, load_sem.at[i])
        for i, (src, dst) in enumerate((
            (vis_hbm, vis_ref), (base_hbm, base_ref), (frac_hbm, frac_ref),
            (tap_hbm, tap_ref), (gain_hbm, gain_ref), (ray_ref, rays.at[0]),
        ))
    ]
    for load in loads:
        load.start()
    barrier = pltpu.get_barrier_semaphore()
    for step in range(1, n):
        pl.semaphore_signal(
            barrier, inc=1, device_id={"link": (me + step) % n}, device_id_type=pl.DeviceIdType.MESH
        )
    for load in loads[:-1]:
        load.wait()
    words = vis_ref[...] * (BASE_SPAN * FRACS) + base_ref[...] * FRACS + frac_ref[...]
    for part in range(slots // LANES):
        meta_own[part] = words[:, part * LANES : (part + 1) * LANES]
    meta_all[0] = meta_own[...]
    elem_all[me, 0:CLUSTERS] = gain_ref[...]
    elem_all[me, CLUSTERS : 2 * CLUSTERS] = (tap_ref[...] & (TAP_SPAN - 1)).astype(F32)
    def expand(first, last):
        def body(index, carry):
            q, user = index // users, index % users
            for part in range(slots // LANES):
                row = meta_all[q, part, pl.ds(user, 1), :]
                ids = lax.shift_right_logical(row, jnp.int32(10))
                square = jnp.transpose(jnp.broadcast_to(ids, (LANES, LANES)))
                at = pl.multiple_of(index * slots + part * LANES, LANES)
                id_cols[pl.ds(at, LANES), :] = square
            return carry

        lax.fori_loop(first, last, body, 0)

    def weigh(first, last):
        def body(index, carry):
            q, user = index // users, index % users
            row = jnp.concatenate(
                [meta_all[q, part, pl.ds(user, 1), :] for part in range(slots // LANES)], axis=1
            )
            frac = (row & (FRACS - 1)).astype(F32) * F32(1.0 / FRACS)
            base = lax.shift_right_logical(row, jnp.int32(4)) & (BASE_SPAN - 1)
            cluster = lax.shift_right_logical(row, jnp.int32(10)) & (CLUSTERS - 1)
            weights = (
                -frac * (frac - 1.0) * (frac - 2.0) / 6.0,
                (frac + 1.0) * (frac - 1.0) * (frac - 2.0) / 2.0,
                -(frac + 1.0) * frac * (frac - 2.0) / 2.0,
                (frac + 1.0) * frac * (frac - 1.0) / 6.0,
            )
            delays = PLACE_ROWS // CLUSTERS
            offset = lax.broadcasted_iota(jnp.int32, (delays, slots), 0) - base
            matrix = jnp.zeros((delays, slots), F32)
            for tap in range(TAPS):
                matrix = jnp.where(offset == tap, weights[tap], matrix)
            top = matrix.astype(BF16).astype(F32)
            member = lax.broadcasted_iota(jnp.int32, (CLUSTERS, slots), 0) == cluster

            def by_cluster(values):
                return jnp.concatenate(
                    [jnp.where(member, values[at : at + 1], F32(0)) for at in range(delays)], axis=0
                ).astype(BF16)

            high, low = by_cluster(top), by_cluster(matrix - top)
            places[index, 0] = high
            places[index, 1] = low
            return carry

        lax.fori_loop(first, last, body, 0)

    picked[...] = jnp.zeros_like(picked)
    expand(0, users)
    pl.semaphore_wait(barrier, n - 1)

    def remote(src, dst, send, recv, target):
        return pltpu.make_async_remote_copy(
            src_ref=src, dst_ref=dst, send_sem=send, recv_sem=recv,
            device_id={"link": target}, device_id_type=pl.DeviceIdType.MESH,
        )

    metas = [
        remote(meta_own, meta_all.at[q], meta_send.at[q], meta_recv.at[q],
               flip(own_set, q, sets) * per_set + place)
        for q in range(1, sets)
    ]
    for copy in metas:
        copy.start()
    elems = [
        remote(elem_all.at[me], elem_all.at[me], elem_send.at[step], elem_recv.at[step],
               (me + step) % n)
        for step in range(1, n)
    ]
    for copy in elems:
        copy.start()

    own_copy = remote(ray_ref, rays.at[1], fwd_send.at[0], fwd_recv.at[0], sibling)
    own_copy.start()

    def far_copy(k):
        return remote(ray_ref, rays.at[2 * k], ray_send.at[k], ray_recv.at[k],
                      own_set * per_set + flip(chip, k, chips) * 2 + core)

    def forward_copy(k):
        return remote(rays.at[2 * k], rays.at[2 * k + 1], fwd_send.at[k], fwd_recv.at[k], sibling)

    far = [far_copy(k) for k in range(1, chips)]
    for copy in far:
        copy.start()
    def prepare(k):
        for other in range(2):
            high, low = split(rays[2 * k + other])
            ray_split[other * owned : (other + 1) * owned, 0:LANES] = high
            ray_split[other * owned : (other + 1) * owned, LANES : 2 * LANES] = low

    def pick(k):
        first = own_set * per_set + flip(chip, k, chips) * 2
        bases = ((first + core) * owned, (first + 1 - core) * owned)

        def body(chunk, carry):
            at = pl.multiple_of(chunk * PICK_ROWS, PICK_ROWS)
            ids = id_cols[pl.ds(at, PICK_ROWS), :]
            lane = lax.broadcasted_iota(jnp.int32, (PICK_ROWS, LANES), 1)
            hot = []
            for start in bases:
                shifted = ids - (lane + start)
                for tile in range(owned // LANES):
                    hot.append(jnp.where(shifted == tile * LANES, F32(1), F32(0)).astype(BF16))
            found = jnp.dot(
                jnp.concatenate(hot, axis=1), ray_split[...], preferred_element_type=F32
            )
            picked[pl.ds(at, PICK_ROWS), :] += found
            return carry

        lax.fori_loop(0, sets * users * slots // PICK_ROWS, body, 0)

    def tabulate():
        owners = LANES // per_dev

        def body(tile, carry):
            both = jnp.concatenate(
                [elem_all[tile * owners + inner] for inner in range(owners)], axis=1
            )
            gain = both[0:CLUSTERS]
            tap = both[CLUSTERS : 2 * CLUSTERS]
            wide = jnp.concatenate(
                [jnp.where(tap == F32(delay), gain, F32(0)) for delay in range(TAP_SPAN)], axis=0
            )
            high, low = split(jnp.transpose(wide))
            at = pl.multiple_of(tile * LANES, LANES)
            depth = TAP_SPAN * CLUSTERS
            table[pl.ds(at, LANES), 0:depth] = high
            table[pl.ds(at, LANES), depth : 2 * depth] = low
            return carry

        lax.fori_loop(0, n // owners, body, 0)

    weigh(0, users)
    for copy in metas:
        copy.wait()
    expand(users, sets * users)
    loads[-1].wait()
    own_copy.wait()
    store = pltpu.make_async_copy(table, table_ref, table_sem)

    def take(k, carry):
        @pl.when(k > 0)
        def _():
            far_copy(k).wait_recv()
            forward = forward_copy(k)
            forward.start()
            forward.wait_recv()

        prepare(k)
        pick(k)

        @pl.when(k == 0)
        def _():
            weigh(users, sets * users)

        @pl.when(k == max(chips - 2, 0))
        def _():
            for copy in elems:
                copy.wait_recv()
            tabulate()
            store.start()

        return carry

    lax.fori_loop(0, chips, take, 0)

    def zones_of(q, pack):
        lane = lax.broadcasted_iota(jnp.int32, (CLUSTERS, LANES), 1)
        shared = jnp.zeros((CLUSTERS, LANES), F32)
        for inner in range(PACK):
            index = q * users + pack * PACK + inner
            rows = picked[pl.ds(pl.multiple_of(index * slots, slots), slots), :].astype(BF16)
            main = jnp.dot(places[index, 0], rows, preferred_element_type=F32)
            rest = jnp.dot(places[index, 1], rows[:, 0:LANES], preferred_element_type=F32)
            stacked = main[:, 0:LANES] + main[:, LANES : 2 * LANES] + rest
            early = stacked[0:CLUSTERS]
            late = jnp.zeros((CLUSTERS, LANES), F32)
            for delay in range(1, BASE_SPAN + TAPS - 1):
                turned = pltpu.roll(
                    stacked[delay * CLUSTERS : (delay + 1) * CLUSTERS], delay, axis=1
                )
                early = early + jnp.where(lane >= delay, turned, F32(0))
                late = late + jnp.where(lane < delay, turned, F32(0))
            zone_part[q, pack, inner * CLUSTERS : (inner + 1) * CLUSTERS, :] = early
            mine = late if inner == 0 else pltpu.roll(late, inner * TAP_SPAN, axis=1)
            inside = (lane >= inner * TAP_SPAN) & (lane < (inner + 1) * TAP_SPAN)
            shared = jnp.where(inside, mine, shared)
        zone_part[q, pack, PACK * CLUSTERS : (PACK + 1) * CLUSTERS, :] = shared

    packs = users // PACK

    def zone_copy(q, pack):
        return remote(zone_part.at[q, pack], zone_got.at[q, pack], zone_send.at[q, pack],
                      zone_recv.at[q, pack], flip(own_set, q, sets) * per_set + place)

    def make(index, carry):
        q, pack = sets - 1 - index // packs, index % packs
        zones_of(q, pack)

        @pl.when(q > 0)
        def _():
            zone_copy(q, pack).start()

        return carry

    lax.fori_loop(0, sets * packs, make, 0)
    for q in range(1, sets):
        for pack in range(packs):
            zone_copy(q, pack).wait()
    total = zone_part[0]
    for q in range(1, sets):
        total = total + zone_got[q]
    zone_ref[...] = total
    store.wait()
    for copy in elems:
        copy.wait_send()
    for k in range(1, chips):
        far_copy(k).wait_send()
        forward_copy(k).wait_send()


def element_kernel(zone_ref, table_ref, out_ref, windows):
    users = zone_ref.shape[0] * PACK
    depth = TAP_SPAN * CLUSTERS

    @pl.when(pl.program_id(0) == 0)
    def _():
        lane = lax.broadcasted_iota(jnp.int32, (CLUSTERS, LANES), 1)
        for user in range(users):
            pack, inner = user // PACK, user % PACK
            early = zone_ref[pack, inner * CLUSTERS : (inner + 1) * CLUSTERS, :]
            late = zone_ref[pack, PACK * CLUSTERS : (PACK + 1) * CLUSTERS, :]
            if inner:
                late = pltpu.roll(late, LANES - inner * TAP_SPAN, axis=1)
            tiles = []
            for delay in range(TAP_SPAN):
                ahead = TAP_SPAN - delay
                tiles.append(pltpu.roll(jnp.where(lane >= ahead, early, late), LANES - ahead, axis=1))
            high, low = split(jnp.concatenate(tiles, axis=0))
            at = user * LANES
            windows[0:depth, at : at + LANES] = high
            windows[depth : 2 * depth, at : at + LANES] = high
            windows[2 * depth : 3 * depth, at : at + LANES] = low

    both = table_ref[...]
    terms = jnp.concatenate([both, both[:, 0:depth]], axis=1)
    for user in range(0, users, 2):
        at = user * LANES
        pair = jnp.dot(terms, windows[:, at : at + 2 * LANES], preferred_element_type=F32)
        out_ref[user] = pair[:, 0:LANES]
        out_ref[user + 1] = pair[:, LANES : 2 * LANES]


def on_device(n, ray_rows, visible, base_tap, frac_index, elem_tap, elem_gain):
    users, slots = visible.shape
    owned = ray_rows.shape[0]
    per_dev = elem_tap.shape[1]
    elements = n * per_dev
    sets = SETS
    per_set = n // sets
    chips = per_set // 2
    dma = pltpu.SemaphoreType.DMA
    vmem = pl.BlockSpec(memory_space=pltpu.VMEM)
    hbm = pl.BlockSpec(memory_space=pl.ANY)
    packs = users // PACK
    depth = TAP_SPAN * CLUSTERS
    packed = ((PACK + 1) * CLUSTERS, LANES)
    zones, table = pl.pallas_call(
        functools.partial(zone_kernel, n, sets),
        out_shape=(
            jax.ShapeDtypeStruct((packs,) + packed, F32),
            jax.ShapeDtypeStruct((elements, 2 * depth), BF16),
        ),
        in_specs=[hbm] * 6,
        out_specs=(vmem, hbm),
        scratch_shapes=[
            pltpu.VMEM((users, slots), jnp.int32),
            pltpu.VMEM((users, slots), jnp.int32),
            pltpu.VMEM((users, slots), jnp.int32),
            pltpu.VMEM((CLUSTERS, per_dev), jnp.int32),
            pltpu.VMEM((CLUSTERS, per_dev), F32),
            pltpu.VMEM((per_set, owned, LANES), F32),
            pltpu.VMEM((n, 2 * CLUSTERS, per_dev), F32),
            pltpu.VMEM((slots // LANES, users, LANES), jnp.int32),
            pltpu.VMEM((sets, slots // LANES, users, LANES), jnp.int32),
            pltpu.VMEM((sets * users * slots, LANES), jnp.int32),
            pltpu.VMEM((2 * owned, 2 * LANES), BF16),
            pltpu.VMEM((sets * users * slots, 2 * LANES), F32),
            pltpu.VMEM((sets * users, 2, PLACE_ROWS, slots), BF16),
            pltpu.VMEM((elements, 2 * depth), BF16),
            pltpu.VMEM((sets, packs) + packed, F32),
            pltpu.VMEM((sets, packs) + packed, F32),
            dma((6,)), dma,
            dma((chips,)), dma((chips,)), dma((chips,)), dma((chips,)),
            dma((sets,)), dma((sets,)), dma((n,)), dma((n,)),
            dma((sets, packs)), dma((sets, packs)),
        ],
        compiler_params=pltpu.CompilerParams(
            collective_id=0, has_side_effects=True, vmem_limit_bytes=56 * 2**20
        ),
        name="zones",
    )(ray_rows, visible, base_tap, frac_index, elem_tap, elem_gain)

    block = 1024
    return pl.pallas_call(
        element_kernel,
        grid=(elements // block,),
        out_shape=jax.ShapeDtypeStruct((users, elements, SAMPLES), F32),
        in_specs=[
            pl.BlockSpec((packs,) + packed, lambda step: (0, 0, 0)),
            pl.BlockSpec((block, 2 * depth), lambda step: (step, 0)),
        ],
        out_specs=pl.BlockSpec((users, block, SAMPLES), lambda step: (0, step, 0)),
        scratch_shapes=[pltpu.VMEM((3 * depth, users * LANES), BF16)],
        compiler_params=pltpu.CompilerParams(vmem_limit_bytes=63 * 2**20),
        name="elements",
    )(zones, table)


def solution(mesh):
    in_specs = (
        P(("group", "link"), None),
        P(("group", "link"), None),
        P(("group", "link"), None),
        P(("group", "link"), None),
        P(None, "link"),
        P(None, "link"),
    )
    out_specs = P(("group", "link"), None, None)
    return jax.shard_map(
        functools.partial(on_device, mesh.shape["link"]),
        mesh=mesh, in_specs=in_specs, out_specs=out_specs, check_vma=False,
    )
```
